32 devices in a mesh: section: 4 (over x, core), dp: 8 (over z, y).
Axes of the slice: x: 2, y: 2, z: 4, core: 2. Of those that a mesh axis runs over, the one named last changes fastest.
Arguments:
- section_inputs: bfloat16 [4, 4, 256, 8192], P('section', None, 'dp'), may hold values from -6 to 6
- adapter_down: bfloat16 [4, 8192, 128], P('section'), may hold values from -0.0625 to 0.0625
- adapter_up: bfloat16 [4, 8192, 128], P('section'), may hold values from -0.5 to 0.5
- representation: bfloat16 [4, 256, 8192], P('section', 'dp'), may hold values from -6 to 6
- head_weights: bfloat16 [8192, 128], P('dp'), may hold values from -1 to 1
- head_targets: bfloat16 [4, 256, 128], P('section', 'dp'), may hold values from -40 to 40
- head_task: int32 [8, 1], replicated, may hold values from 0 to 5
Outputs:
- down_grads: float32 [4, 8192, 128], P('section', 'dp')
- up_grads: float32 [4, 8192, 128], P('section', 'dp')
- task_weights: float32 [6], replicated
The draws below stay inside these ranges and needn't reach their ends.
Inputs may be any that keep to these rules, and one draw needn't show every extreme that they name: `head_task`: each head belongs to one task, and every task has at least one head.
All inputs are finite; a program needn't handle non-finite values.
Results may differ from the reference program's by a relative error of at most 0.022.
Values may be sent and summed in bfloat16 or wider, within the bound.
A program may use at most 64 MiB of HBM per device.

```python
import jax
import jax.numpy as jnp
from jax import lax

D = 8192
RANK = 128
HEADS = 8
HEAD_OUT = 16
TASKS = 6
STEPS = 20
MICRO = 4
TOKENS = 256
N_SECTION = 4


def draw_head_weights(key, part):
    key_common, key_own = jax.random.split(key)
    columns = HEADS * HEAD_OUT
    common = jax.random.normal(key_common, (D, HEAD_OUT), jnp.float32)
    own_part = jax.random.normal(key_own, (D, columns), jnp.float32)
    tiled_common = jnp.tile(common, (1, HEADS))
    values = (0.8 * tiled_common + 0.6 * own_part) / jnp.sqrt(jnp.float32(D))
    return jnp.clip(values, -1.0, 1.0).astype(jnp.bfloat16)


def draw_head_targets(key, part):
    subkeys = jax.random.split(key, 4)
    columns = HEADS * HEAD_OUT
    full_shape = (MICRO, TOKENS, columns)
    position = (jnp.arange(MICRO * TOKENS, dtype=jnp.float32) / (MICRO * TOKENS)).reshape(MICRO, TOKENS, 1)
    rising = 0.5 * jnp.exp(jnp.log(4.0) * position)
    token_scale = jnp.exp(jax.random.uniform(subkeys[0], (MICRO, TOKENS, 1), jnp.float32, -0.693, 0.693))
    shared = jax.random.normal(subkeys[1], (MICRO, TOKENS, HEAD_OUT), jnp.float32)
    own_part = jax.random.normal(subkeys[2], full_shape, jnp.float32)
    column_scale = jnp.exp(jax.random.uniform(subkeys[3], (1, 1, columns), jnp.float32, -0.693, 0.693))
    values = rising * token_scale * column_scale * (0.6 * jnp.tile(shared, (1, 1, HEADS)) + 0.8 * own_part)
    return jnp.clip(values, -40.0, 40.0).astype(jnp.bfloat16)


def block_scale(stream_key, shape, cuts, least, high):
    factor_of = 1.0
    for dim, shards_of in cuts:
        draws = jax.random.uniform(jax.random.fold_in(jax.random.fold_in(stream_key, 6), dim), (shards_of,), jnp.float32, least / len(cuts), high / len(cuts))
        factor_of = factor_of * jnp.repeat(jnp.exp(draws), shape[dim] // shards_of).reshape((-1,) + (1,) * (len(shape) - 1 - dim))
    return factor_of


def different_ones(stream_key, rows, amount, top, lift):
    sequence = jax.random.permutation(jax.random.fold_in(stream_key, 1), amount)
    boost = sequence
    for power in range(3):
        boost = boost * boost // amount
    boost = boost * lift // amount
    tickets = jax.random.randint(jax.random.fold_in(stream_key, 2), (rows, amount), 0, 4096) + boost
    sure = jax.random.permutation(jax.random.fold_in(stream_key, 3), rows)[jnp.arange(amount) % rows]
    tickets = jnp.where(jnp.arange(rows)[:, None] == sure[None, :], 1 << 14, tickets)
    merit = tickets * amount + jnp.arange(amount)
    return lax.top_k(merit.astype(jnp.int32), top)[1].astype(jnp.int32)


def noise(stream_key, shape, width, most, cuts=(), kind=jnp.bfloat16):
    array = width * jax.random.normal(stream_key, shape, jnp.float32)
    if cuts:
        array = array * block_scale(stream_key, shape, cuts, -0.22, 0.18)
    return jnp.clip(array, -most, most).astype(kind)


def setup_inputs(seed: int = 0) -> dict:
    arg_keys = jax.random.split(jax.random.key(seed), 8)
    section_inputs = noise(arg_keys[0], (N_SECTION, MICRO, TOKENS, D), 1.0, 6.0, ((0, 4), (2, 8)))
    adapter_down = noise(arg_keys[1], (N_SECTION, D, RANK), D ** -0.5, 0.0625, ((0, 4),))
    adapter_up = noise(arg_keys[2], (N_SECTION, D, RANK), RANK ** -0.5, 0.5, ((0, 4),))
    representation = noise(arg_keys[3], (MICRO, TOKENS, D), 1.0, 6.0, ((0, 4), (1, 8)))
    head_weights = draw_head_weights(jax.random.fold_in(arg_keys[7], 71), 0)
    head_targets = draw_head_targets(jax.random.fold_in(arg_keys[7], 71), 0)
    head_task = different_ones(arg_keys[6], HEADS, TASKS, 1, 0)
    return {"section_inputs": section_inputs, "adapter_down": adapter_down, "adapter_up": adapter_up, "representation": representation, "head_weights": head_weights, "head_targets": head_targets, "head_task": head_task}


STEP_RATE = 3.0


def swish_slope(preact):
    logistic = jax.nn.sigmoid(preact)
    return logistic * (1.0 + preact * (1.0 - logistic))


def task_matrix(head_task):
    column_task = jnp.repeat(head_task[:, 0], HEAD_OUT)
    return (column_task[None, :] == jnp.arange(TASKS, dtype=jnp.int32)[:, None]).astype(jnp.float32)


def descend(gram_matrix):
    trace_sum = jnp.trace(gram_matrix) + 1e-6
    start = jnp.full((TASKS,), 1.0 / TASKS, dtype=jnp.float32)

    def advance(counter, weights):
        descent = jnp.dot(gram_matrix, weights, precision=lax.Precision.HIGHEST) / trace_sum
        weights = weights * jnp.exp(-STEP_RATE * descent)
        return weights / jnp.sum(weights)

    return lax.fori_loop(0, STEPS, advance, start)


def section_back(inputs, down_map, up_map, cotangent):
    preact = jnp.dot(inputs, down_map, preferred_element_type=jnp.float32)
    active = jax.nn.silu(preact).astype(jnp.bfloat16)
    branch = jnp.dot(cotangent, up_map, preferred_element_type=jnp.float32)
    inner = (branch * swish_slope(preact)).astype(jnp.bfloat16)
    back = lax.dot_general(inner, down_map, (((1,), (1,)), ((), ())), preferred_element_type=jnp.float32)
    passed = (cotangent.astype(jnp.float32) + back).astype(jnp.bfloat16)
    return active, inner, passed


def reference(section_inputs, adapter_down, adapter_up, representation, head_weights, head_targets, head_task):
    onehot = task_matrix(head_task)
    residuals = []
    gram_matrix = jnp.zeros((TASKS, TASKS), jnp.float32)
    for micro_index in range(MICRO):
        predicted = jnp.dot(representation[micro_index], head_weights, preferred_element_type=jnp.float32)
        residual = (predicted - head_targets[micro_index].astype(jnp.float32)).astype(jnp.bfloat16)
        residuals.append(residual)
        task_grads = jnp.stack([lax.dot_general(residual * onehot[task_index].astype(jnp.bfloat16), head_weights, (((1,), (1,)), ((), ())), preferred_element_type=jnp.float32) for task_index in range(TASKS)])
        gram_matrix = gram_matrix + jnp.einsum('atd,btd->ab', task_grads, task_grads, precision=lax.Precision.HIGHEST)
    mixing = descend(gram_matrix)
    column_weight = jnp.dot(mixing, onehot, precision=lax.Precision.HIGHEST)
    cotangents = []
    for residual in residuals:
        weighted = (residual.astype(jnp.float32) * column_weight[None, :]).astype(jnp.bfloat16)
        cotangents.append(lax.dot_general(weighted, head_weights, (((1,), (1,)), ((), ())), preferred_element_type=jnp.float32).astype(jnp.bfloat16))
    down_list = []
    up_list = []
    for section_index in range(N_SECTION - 1, -1, -1):
        grad_down = jnp.zeros((D, RANK), jnp.float32)
        grad_up = jnp.zeros((D, RANK), jnp.float32)
        for micro_index in range(MICRO):
            inputs = section_inputs[section_index, micro_index]
            current = cotangents[micro_index]
            active, inner, passed = section_back(inputs, adapter_down[section_index], adapter_up[section_index], current)
            grad_down = grad_down + jnp.dot(inputs.T, inner, preferred_element_type=jnp.float32)
            grad_up = grad_up + jnp.dot(current.T, active, preferred_element_type=jnp.float32)
            cotangents[micro_index] = passed
        down_list.insert(0, grad_down)
        up_list.insert(0, grad_up)
    return jnp.stack(down_list), jnp.stack(up_list), mixing
```

```python
import functools

import jax
import jax.numpy as jnp
from jax import lax
from jax.experimental import pallas as pl
from jax.experimental.pallas import tpu as pltpu
from jax.sharding import PartitionSpec as P

TASKS = 6
STEPS = 20
STEP_RATE = 3.0
TASK_ROWS = 8

REP, XIN, PRED, KSUM, KALL, GRAM, INNER, TSUM, TALL = range(9)
DOWN, RESID, CHAIN = range(3)

F32 = jnp.float32
BF16 = jnp.bfloat16


def round_up(value, unit):
    return -(-value // unit) * unit


def mm(a, b, precision=None):
    return jnp.dot(a, b, preferred_element_type=F32, precision=precision)


def mm_t(a, b):
    return lax.dot_general(a, b, (((0,), (0,)), ((), ())), preferred_element_type=F32)


def kernel(
    sections, peers, heads,
    x_hbm, down_hbm, up_hbm, rep_hbm, w_hbm, targets, head_task,
    down_out, up_out, mix_out,
    x_buf, down_buf, up_buf, basis, repg, xg, pred, predg, kpart, kslots, kall,
    resid, gpart, gslots, inner, innerg, tpart, tslots, tsum, active, slope, branch,
    local_sem, dp_send, dp_recv, sec_send, sec_recv,
):
    rows, width = x_buf.shape
    rank = down_buf.shape[1]
    block = width // peers
    toks = repg.shape[1]
    krows = kslots.shape[1]
    trows = tslots.shape[1]
    me = lax.axis_index("dp")
    sec = lax.axis_index("section")

    def columns(index):
        return pl.ds(pl.multiple_of(index * block, block), block)

    def blocks(index):
        return pl.ds(pl.multiple_of(index * block, block), block)

    def dp_copy(ex, src, dst, slot, peer):
        return pltpu.make_async_remote_copy(
            src_ref=src, dst_ref=dst, send_sem=dp_send.at[ex, peer], recv_sem=dp_recv.at[ex, slot],
            device_id={"dp": peer}, device_id_type=pl.DeviceIdType.MESH,
        )

    def sec_copy(ex, src, dst, slot, peer):
        return pltpu.make_async_remote_copy(
            src_ref=src, dst_ref=dst, send_sem=sec_send.at[ex, peer], recv_sem=sec_recv.at[ex, slot],
            device_id={"section": peer}, device_id_type=pl.DeviceIdType.MESH,
        )

    def each_dp(action):
        @pl.loop(1, peers)
        def _(k):
            action(lax.rem(me + k, peers))

    def each_sec(action):
        @pl.loop(1, sections)
        def _(k):
            action(lax.rem(sec + k, sections))

    def dp_start(ex, src_of, dst):
        each_dp(lambda peer: dp_copy(ex, src_of(peer), dst, me, peer).start())

    def dp_wait(ex, dst_of):
        each_dp(lambda peer: dp_copy(ex, dst_of(peer), dst_of(peer), peer, peer).wait_recv())

    def dp_sent(ex, src_of):
        each_dp(lambda peer: dp_copy(ex, src_of(peer), src_of(peer), peer, peer).wait_send())

    def sec_start(ex, src, dst):
        each_sec(lambda peer: sec_copy(ex, src, dst, sec, peer).start())

    def sec_wait(ex, dst_of):
        each_sec(lambda peer: sec_copy(ex, dst_of(peer), dst_of(peer), peer, peer).wait_recv())

    def sec_sent(ex, src):
        each_sec(lambda peer: sec_copy(ex, src, src, peer, peer).wait_send())

    my_block = blocks(me)
    local = [
        pltpu.make_async_copy(rep_hbm.at[:, columns(me)], repg.at[me], local_sem.at[0]),
        pltpu.make_async_copy(w_hbm, basis.at[sec], local_sem.at[1]),
        pltpu.make_async_copy(x_hbm, x_buf, local_sem.at[2]),
        pltpu.make_async_copy(down_hbm, down_buf, local_sem.at[3]),
        pltpu.make_async_copy(up_hbm.at[my_block], up_buf, local_sem.at[4]),
        pltpu.make_async_copy(x_hbm.at[:, columns(me)], xg.at[me], local_sem.at[5]),
    ]
    for copy in local:
        copy.start()

    barrier = pltpu.get_barrier_semaphore()
    each_dp(lambda peer: pl.semaphore_signal(
        barrier, inc=1, device_id={"dp": peer}, device_id_type=pl.DeviceIdType.MESH))
    each_sec(lambda peer: pl.semaphore_signal(
        barrier, inc=1, device_id={"section": peer}, device_id_type=pl.DeviceIdType.MESH))
    pl.semaphore_wait(barrier, peers + sections - 2)

    dp_start(REP, lambda peer: rep_hbm.at[:, columns(peer)], repg.at[me])
    sec_start(DOWN, down_hbm.at[my_block], basis.at[sec])
    dp_start(XIN, lambda peer: x_hbm.at[:, columns(peer)], xg.at[me])

    local[2].wait()
    local[3].wait()

    def add_preact(k, total):
        return total + mm(x_buf[:, columns(k)], down_buf[blocks(k), :])

    preact = lax.fori_loop(0, peers, add_preact, jnp.zeros((rows, rank), F32))
    logistic = jax.nn.sigmoid(preact)
    active[...] = (preact * logistic).astype(BF16)
    slope[...] = logistic * (1.0 + preact * (1.0 - logistic))

    local[0].wait()
    local[1].wait()
    dp_wait(REP, lambda peer: repg.at[peer])
    head_block = basis[sec]

    @pl.loop(0, peers)
    def _(n):
        pred[n] = mm(repg[n], head_block)

    dp_start(PRED, lambda peer: pred.at[peer], predg.at[me])
    predg[me] = pred[me]

    local[4].wait()
    sec_wait(DOWN, lambda peer: basis.at[peer])
    used = (sections + 1) * rank
    if kpart.shape[0] > used:
        kpart[used:, :] = jnp.zeros((kpart.shape[0] - used, rank), F32)
    up_block = up_buf[...]
    for j in range(sections):
        kpart[j * rank : (j + 1) * rank, :] = mm_t(basis[j], up_block)
    kpart[sections * rank : used, :] = mm_t(head_block, head_block)

    def kspan(index):
        return pl.ds(pl.multiple_of(index * krows, 8), krows)

    dp_start(KSUM, lambda peer: kpart.at[kspan(peer)], kslots.at[me])
    kslots[me] = kpart[kspan(me), :]

    dp_wait(PRED, lambda peer: predg.at[peer])
    predicted = lax.fori_loop(1, peers, lambda n, total: total + predg[n], predg[0])
    resid[sec] = (predicted - targets[...].astype(F32)).astype(BF16)
    sec_start(RESID, resid.at[sec], resid.at[sec])

    dp_wait(KSUM, lambda peer: kslots.at[peer])
    kall[kspan(me), :] = lax.fori_loop(1, peers, lambda n, total: total + kslots[n], kslots[0])
    dp_start(KALL, lambda peer: kall.at[kspan(me)], kall.at[kspan(me)])

    lanes = lax.broadcasted_iota(jnp.int32, (heads, rank), 1)
    owner = lax.broadcasted_iota(jnp.int32, (heads, rank), 0) * (rank // heads)
    of_head = (lanes >= owner) & (lanes < owner + rank // heads)
    column_task = jnp.sum(
        jnp.where(of_head, head_task[...].astype(F32), 0.0), axis=0, keepdims=True
    )
    wide = lax.broadcasted_iota(jnp.int32, (rank, rank), 0).astype(F32)
    task_wide = (wide == column_task).astype(F32)
    task_tall = task_wide[:TASK_ROWS]

    sec_wait(RESID, lambda peer: resid.at[peer])
    tokens = resid[...].reshape(rows, rank)
    outer = mm_t(tokens, tokens)
    dp_wait(KALL, lambda peer: kall.at[kspan(peer)])
    product = outer * kall[sections * rank : used, :]
    half = mm(task_tall, product, lax.Precision.HIGHEST)
    share = lax.dot_general(
        half, task_wide, (((1,), (1,)), ((), ())),
        preferred_element_type=F32, precision=lax.Precision.HIGHEST,
    )
    gpart[...] = share
    gslots[me] = share
    dp_start(GRAM, lambda peer: gpart, gslots.at[me])
    dp_wait(GRAM, lambda peer: gslots.at[peer])
    gram = lax.fori_loop(1, peers, lambda n, total: total + gslots[n], gslots[0])

    down_index = lax.broadcasted_iota(jnp.int32, gram.shape, 0)
    lane_index = lax.broadcasted_iota(jnp.int32, gram.shape, 1)
    trace = jnp.sum(
        jnp.sum(jnp.where(down_index == lane_index, gram, 0.0), axis=1, keepdims=True),
        axis=0, keepdims=True,
    ) + 1e-6
    scaled = gram * (-STEP_RATE / trace)
    tall = jnp.where(down_index[:, :1] < TASKS, 1.0 / TASKS, 0.0).astype(F32)
    flat = jnp.where(lane_index[:1] < TASKS, 1.0 / TASKS, 0.0).astype(F32)
    for _ in range(STEPS):
        along = jnp.sum(scaled * tall, axis=0, keepdims=True)
        across = jnp.sum(scaled * flat, axis=1, keepdims=True)
        tall = tall * jnp.exp(across)
        flat = flat * jnp.exp(along)
        inverse = 1.0 / jnp.sum(tall, axis=0, keepdims=True)
        tall = tall * inverse
        flat = flat * inverse
    mix_out[...] = jnp.broadcast_to(flat, mix_out.shape)

    column_weight = jnp.sum(task_tall * tall, axis=0, keepdims=True)
    weighted = (tokens.astype(F32) * column_weight).astype(BF16)

    def kmat(index):
        return kall[pl.ds(pl.multiple_of(index * rank, rank), rank), :].astype(BF16)

    def tspan(index):
        return pl.ds(pl.multiple_of(index * trows, 16), trows)

    def tmat(index):
        return pl.ds(pl.multiple_of(index * rank, rank), rank)

    tpart[...] = jnp.zeros(tpart.shape, BF16)
    tpart[tmat(sec), :] = mm_t(weighted, active[...]).astype(BF16)
    branch[...] = mm(weighted, kmat(sec))
    for j in range(sections - 1, -1, -1):
        @pl.when(sec == j)
        def _():
            inner[j] = (branch[...] * slope[...]).astype(BF16)
            for lower in range(j):
                sec_copy(CHAIN, inner.at[j], inner.at[j], j, lower).start()

        @pl.when(sec < j)
        def _():
            sec_copy(CHAIN, inner.at[j], inner.at[j], j, j).wait_recv()
            branch[...] += mm(inner[j], kmat(j))
            tpart[j * rank : (j + 1) * rank, :] = mm_t(inner[j], active[...]).astype(BF16)

    dp_start(TSUM, lambda peer: tpart.at[tspan(peer)], tslots.at[me])
    dp_start(INNER, lambda peer: inner.at[sec], innerg.at[me])
    tslots[me] = tpart[tspan(me), :]
    innerg[me] = inner[sec]

    dp_wait(TSUM, lambda peer: tslots.at[peer])
    tsum[tspan(me), :] = lax.fori_loop(
        1, peers, lambda n, total: total + tslots[n].astype(F32), tslots[0].astype(F32)
    ).astype(BF16)
    dp_start(TALL, lambda peer: tsum.at[tspan(me)], tsum.at[tspan(me)])

    local[5].wait()
    dp_wait(INNER, lambda peer: innerg.at[peer])
    dp_wait(XIN, lambda peer: xg.at[peer])
    down_out[...] = jnp.zeros(down_out.shape, F32)

    @pl.loop(0, peers)
    def _(n):
        down_out[...] += mm_t(xg[n], innerg[n])

    dp_wait(TALL, lambda peer: tsum.at[tspan(peer)])
    up_out[...] = mm(basis[0], tsum[:rank, :])

    @pl.loop(1, sections)
    def _(n):
        up_out[...] += mm(basis[n], tsum[tmat(n), :])

    dp_sent(REP, lambda peer: repg.at[me])
    dp_sent(XIN, lambda peer: xg.at[me])
    dp_sent(PRED, lambda peer: pred.at[peer])
    dp_sent(KSUM, lambda peer: kpart.at[kspan(peer)])
    dp_sent(KALL, lambda peer: kall.at[kspan(me)])
    dp_sent(GRAM, lambda peer: gpart)
    dp_sent(INNER, lambda peer: inner.at[sec])
    dp_sent(TSUM, lambda peer: tpart.at[tspan(peer)])
    dp_sent(TALL, lambda peer: tsum.at[tspan(me)])
    sec_sent(DOWN, basis.at[sec])
    sec_sent(RESID, resid.at[sec])
    for j in range(1, sections):
        @pl.when(sec == j)
        def _():
            for lower in range(j):
                sec_copy(CHAIN, inner.at[j], inner.at[j], lower, lower).wait_send()


def body(
    section_inputs, adapter_down, adapter_up, representation, head_weights, head_targets, head_task
):
    sections = lax.axis_size("section")
    peers = lax.axis_size("dp")
    _, micro, toks, width = section_inputs.shape
    rank = adapter_down.shape[2]
    rows = micro * toks
    block = width // peers
    krows = round_up(-(-(sections + 1) * rank // peers), 16)
    trows = round_up(-(-sections * rank // peers), 16)
    vmem = pl.BlockSpec(memory_space=pltpu.VMEM)
    hbm = pl.BlockSpec(memory_space=pl.ANY)
    scratch = [
        pltpu.VMEM((rows, width), BF16),
        pltpu.VMEM((width, rank), BF16),
        pltpu.VMEM((block, rank), BF16),
        pltpu.VMEM((sections, block, rank), BF16),
        pltpu.VMEM((peers, toks, block), BF16),
        pltpu.VMEM((peers, rows, block), BF16),
        pltpu.VMEM((peers, toks, rank), F32),
        pltpu.VMEM((peers, toks, rank), F32),
        pltpu.VMEM((peers * krows, rank), F32),
        pltpu.VMEM((peers, krows, rank), F32),
        pltpu.VMEM((peers * krows, rank), F32),
        pltpu.VMEM((sections, toks, rank), BF16),
        pltpu.VMEM((TASK_ROWS, rank), F32),
        pltpu.VMEM((peers, TASK_ROWS, rank), F32),
        pltpu.VMEM((sections, rows, rank), BF16),
        pltpu.VMEM((peers, rows, rank), BF16),
        pltpu.VMEM((peers * trows, rank), BF16),
        pltpu.VMEM((peers, trows, rank), BF16),
        pltpu.VMEM((peers * trows, rank), BF16),
        pltpu.VMEM((rows, rank), BF16),
        pltpu.VMEM((rows, rank), F32),
        pltpu.VMEM((rows, rank), F32),
        pltpu.SemaphoreType.DMA((6,)),
        pltpu.SemaphoreType.DMA((9, peers)),
        pltpu.SemaphoreType.DMA((9, peers)),
        pltpu.SemaphoreType.DMA((3, sections)),
        pltpu.SemaphoreType.DMA((3, sections)),
    ]
    down, up, mix = pl.pallas_call(
        functools.partial(kernel, sections, peers, head_task.shape[0]),
        out_shape=(
            jax.ShapeDtypeStruct((block, rank), F32),
            jax.ShapeDtypeStruct((block, rank), F32),
            jax.ShapeDtypeStruct((TASK_ROWS, rank), F32),
        ),
        in_specs=[hbm] * 5 + [vmem] * 2,
        out_specs=(vmem, vmem, vmem),
        scratch_shapes=scratch,
        compiler_params=pltpu.CompilerParams(
            collective_id=0, has_side_effects=True, vmem_limit_bytes=48 << 20
        ),
    )(
        section_inputs.reshape(rows, width), adapter_down[0], adapter_up[0], representation[0],
        head_weights, head_targets[0], head_task,
    )
    return (down[None], up[None], mix[0, :TASKS])


def solution(mesh):
    in_specs = (
        P("section", None, "dp", None),
        P("section", None, None),
        P("section", None, None),
        P("section", "dp", None),
        P("dp", None),
        P("section", "dp", None),
        P(),
    )
    out_specs = (P("section", "dp", None), P("section", "dp", None), P())
    return jax.shard_map(body, mesh=mesh, in_specs=in_specs, out_specs=out_specs, check_vma=False)
```

```python
import functools

import jax
import jax.numpy as jnp
from jax import lax
from jax.experimental import pallas as pl
from jax.experimental.pallas import tpu as pltpu
from jax.sharding import PartitionSpec as P

TASKS = 6
STEPS = 20
STEP_RATE = 3.0
TASK_ROWS = 8

REP, PRED, KSUM, KALL, WSUM, WALL, GRAM, TSUM, TALL = range(9)
XOWN, XFAR, INNER = range(3)
DOWN, RESID, CHAIN = range(3)

F32 = jnp.float32
BF16 = jnp.bfloat16


def round_up(value, unit):
    return -(-value // unit) * unit


def mm(a, b, precision=None):
    return jnp.dot(a, b, preferred_element_type=F32, precision=precision)


def mm_t(a, b):
    return lax.dot_general(a, b, (((0,), (0,)), ((), ())), preferred_element_type=F32)


def kernel(
    sections, peers, heads,
    x_hbm, down_hbm, up_hbm, rep_hbm, w_hbm, targets, head_task,
    down_out, up_out, mix_out,
    x_buf, down_buf, up_buf, basis, repg, xg, pred, predg, kpart, kslots, kall, wpart, wslots, wall,
    resid, gpart, gslots, inner, innerg, tpart, tslots, tsum, active, slope, branch, cross, crossg,
    local_sem, dp_send, dp_recv, half_send, half_recv, far_send, far_recv, sec_send, sec_recv,
):
    rows, width = x_buf.shape
    rank = down_buf.shape[1]
    block = width // peers
    toks = repg.shape[1]
    krows = kslots.shape[1]
    wrows = wslots.shape[1]
    half = peers // 2
    trows = tslots.shape[1]
    me = lax.axis_index("dp")
    sec = lax.axis_index("section")
    first = lax.div(me, half) * half
    place = me - first
    far = lax.rem(me + half, peers)

    def columns(index):
        return pl.ds(pl.multiple_of(index * block, block), block)

    def blocks(index):
        return pl.ds(pl.multiple_of(index * block, block), block)

    def dp_copy(ex, src, dst, slot, peer):
        return pltpu.make_async_remote_copy(
            src_ref=src, dst_ref=dst, send_sem=dp_send.at[ex, peer], recv_sem=dp_recv.at[ex, slot],
            device_id={"dp": peer}, device_id_type=pl.DeviceIdType.MESH,
        )

    def sec_copy(ex, src, dst, slot, peer):
        return pltpu.make_async_remote_copy(
            src_ref=src, dst_ref=dst, send_sem=sec_send.at[ex, peer], recv_sem=sec_recv.at[ex, slot],
            device_id={"section": peer}, device_id_type=pl.DeviceIdType.MESH,
        )

    def half_copy(ex, src, dst, slot, peer):
        return pltpu.make_async_remote_copy(
            src_ref=src, dst_ref=dst, send_sem=half_send.at[ex, peer], recv_sem=half_recv.at[ex, slot],
            device_id={"dp": first + peer}, device_id_type=pl.DeviceIdType.MESH,
        )

    def far_copy(part):
        return pltpu.make_async_remote_copy(
            src_ref=cross.at[part], dst_ref=crossg.at[part], send_sem=far_send.at[part],
            recv_sem=far_recv.at[part], device_id={"dp": far}, device_id_type=pl.DeviceIdType.MESH,
        )

    def each_half(action):
        @pl.loop(1, half)
        def _(k):
            action(lax.rem(place + k, half))

    def send_inputs(k):
        peer = lax.rem(place + k, half)
        half_copy(XOWN, x_hbm.at[:, columns(first + peer)], xg.at[0, place], place, peer).start()
        beyond = lax.rem(first + peer + half, peers)
        half_copy(XFAR, x_hbm.at[:, columns(beyond)], xg.at[1, place], place, peer).start()

    def each_dp(action):
        @pl.loop(1, peers)
        def _(k):
            action(lax.rem(me + k, peers))

    def each_sec(action):
        @pl.loop(1, sections)
        def _(k):
            action(lax.rem(sec + k, sections))

    def dp_start(ex, src_of, dst):
        each_dp(lambda peer: dp_copy(ex, src_of(peer), dst, me, peer).start())

    def dp_wait(ex, dst_of):
        each_dp(lambda peer: dp_copy(ex, dst_of(peer), dst_of(peer), peer, peer).wait_recv())

    def dp_sent(ex, src_of):
        each_dp(lambda peer: dp_copy(ex, src_of(peer), src_of(peer), peer, peer).wait_send())

    def sec_start(ex, src, dst):
        each_sec(lambda peer: sec_copy(ex, src, dst, sec, peer).start())

    def sec_wait(ex, dst_of):
        each_sec(lambda peer: sec_copy(ex, dst_of(peer), dst_of(peer), peer, peer).wait_recv())

    def sec_sent(ex, src):
        each_sec(lambda peer: sec_copy(ex, src, src, peer, peer).wait_send())

    my_block = blocks(me)
    local = [
        pltpu.make_async_copy(rep_hbm.at[:, columns(me)], repg.at[me], local_sem.at[0]),
        pltpu.make_async_copy(w_hbm, basis.at[sec], local_sem.at[1]),
        pltpu.make_async_copy(x_hbm, x_buf, local_sem.at[2]),
        pltpu.make_async_copy(down_hbm, down_buf, local_sem.at[3]),
        pltpu.make_async_copy(up_hbm.at[my_block], up_buf, local_sem.at[4]),
        pltpu.make_async_copy(x_hbm.at[:, columns(me)], xg.at[0, place], local_sem.at[5]),
        pltpu.make_async_copy(x_hbm.at[:, columns(far)], xg.at[1, place], local_sem.at[6]),
    ]
    for copy in local:
        copy.start()

    barrier = pltpu.get_barrier_semaphore()
    each_dp(lambda peer: pl.semaphore_signal(
        barrier, inc=1, device_id={"dp": peer}, device_id_type=pl.DeviceIdType.MESH))
    each_sec(lambda peer: pl.semaphore_signal(
        barrier, inc=1, device_id={"section": peer}, device_id_type=pl.DeviceIdType.MESH))
    pl.semaphore_wait(barrier, peers + sections - 2)

    dp_start(REP, lambda peer: rep_hbm.at[:, columns(peer)], repg.at[me])
    sec_start(DOWN, down_hbm.at[my_block], basis.at[sec])

    local[1].wait()
    head_block = basis[sec]
    if wpart.shape[0] > rank:
        wpart[rank:, :] = jnp.zeros((wpart.shape[0] - rank, rank), F32)
    wpart[:rank, :] = mm_t(head_block, head_block)

    def wspan(index):
        return pl.ds(pl.multiple_of(index * wrows, 8), wrows)

    dp_start(WSUM, lambda peer: wpart.at[wspan(peer)], wslots.at[me])
    wslots[me] = wpart[wspan(me), :]

    cuts = [1 + (half - 1) * part // 3 for part in range(4)]

    def send_part(part):
        for k in range(cuts[part], cuts[part + 1]):
            send_inputs(k)

    send_part(0)

    local[2].wait()
    local[3].wait()

    def add_preact(k, total):
        return total + mm(x_buf[:, columns(k)], down_buf[blocks(k), :])

    preact = lax.fori_loop(0, peers, add_preact, jnp.zeros((rows, rank), F32))
    logistic = jax.nn.sigmoid(preact)
    active[...] = (preact * logistic).astype(BF16)
    slope[...] = logistic * (1.0 + preact * (1.0 - logistic))

    local[0].wait()
    dp_wait(REP, lambda peer: repg.at[peer])

    @pl.loop(0, peers)
    def _(n):
        pred[n] = mm(repg[n], head_block)

    dp_start(PRED, lambda peer: pred.at[peer], predg.at[me])
    predg[me] = pred[me]
    dp_wait(WSUM, lambda peer: wslots.at[peer])
    wall[wspan(me), :] = lax.fori_loop(1, peers, lambda n, total: total + wslots[n], wslots[0])
    dp_start(WALL, lambda peer: wall.at[wspan(me)], wall.at[wspan(me)])
    send_part(1)

    local[4].wait()
    sec_wait(DOWN, lambda peer: basis.at[peer])
    used = sections * rank
    if kpart.shape[0] > used:
        kpart[used:, :] = jnp.zeros((kpart.shape[0] - used, rank), BF16)
    up_block = up_buf[...].T
    for j in range(sections):
        kpart[j * rank : (j + 1) * rank, :] = mm(up_block, basis[j]).astype(BF16)

    def kspan(index):
        return pl.ds(pl.multiple_of(index * krows, 16), krows)

    dp_start(KSUM, lambda peer: kpart.at[kspan(peer)], kslots.at[me])
    kslots[me] = kpart[kspan(me), :]

    dp_wait(PRED, lambda peer: predg.at[peer])
    predicted = lax.fori_loop(1, peers, lambda n, total: total + predg[n], predg[0])
    resid[sec] = (predicted - targets[...].astype(F32)).astype(BF16)
    sec_start(RESID, resid.at[sec], resid.at[sec])
    send_part(2)

    dp_wait(KSUM, lambda peer: kslots.at[peer])
    kall[kspan(me), :] = lax.fori_loop(
        1, peers, lambda n, total: total + kslots[n].astype(F32), kslots[0].astype(F32)
    ).astype(BF16)
    dp_start(KALL, lambda peer: kall.at[kspan(me)], kall.at[kspan(me)])

    lanes = lax.broadcasted_iota(jnp.int32, (heads, rank), 1)
    owner = lax.broadcasted_iota(jnp.int32, (heads, rank), 0) * (rank // heads)
    of_head = (lanes >= owner) & (lanes < owner + rank // heads)
    column_task = jnp.sum(
        jnp.where(of_head, head_task[...].astype(F32), 0.0), axis=0, keepdims=True
    )
    wide = lax.broadcasted_iota(jnp.int32, (rank, rank), 0).astype(F32)
    task_wide = (wide == column_task).astype(F32)
    task_tall = task_wide[:TASK_ROWS]

    sec_wait(RESID, lambda peer: resid.at[peer])
    tokens = resid[...].reshape(rows, rank)
    outer = mm_t(tokens, tokens)
    dp_wait(WALL, lambda peer: wall.at[wspan(peer)])
    product = outer * wall[:rank, :]
    picked = mm(task_tall, product, lax.Precision.HIGHEST)
    share = lax.dot_general(
        picked, task_wide, (((1,), (1,)), ((), ())),
        preferred_element_type=F32, precision=lax.Precision.HIGHEST,
    )
    gpart[...] = share
    gslots[me] = share
    dp_start(GRAM, lambda peer: gpart, gslots.at[me])
    dp_wait(GRAM, lambda peer: gslots.at[peer])
    gram = lax.fori_loop(1, peers, lambda n, total: total + gslots[n], gslots[0])

    down_index = lax.broadcasted_iota(jnp.int32, gram.shape, 0)
    lane_index = lax.broadcasted_iota(jnp.int32, gram.shape, 1)
    trace = jnp.sum(
        jnp.sum(jnp.where(down_index == lane_index, gram, 0.0), axis=1, keepdims=True),
        axis=0, keepdims=True,
    ) + 1e-6
    scaled = gram * (-STEP_RATE / trace)
    tall = jnp.where(down_index[:, :1] < TASKS, 1.0 / TASKS, 0.0).astype(F32)
    flat = jnp.where(lane_index[:1] < TASKS, 1.0 / TASKS, 0.0).astype(F32)
    for _ in range(STEPS):
        along = jnp.sum(scaled * tall, axis=0, keepdims=True)
        across = jnp.sum(scaled * flat, axis=1, keepdims=True)
        tall = tall * jnp.exp(across)
        flat = flat * jnp.exp(along)
        inverse = 1.0 / jnp.sum(tall, axis=0, keepdims=True)
        tall = tall * inverse
        flat = flat * inverse
    mix_out[...] = jnp.broadcast_to(flat, mix_out.shape)

    dp_wait(KALL, lambda peer: kall.at[kspan(peer)])

    column_weight = jnp.sum(task_tall * tall, axis=0, keepdims=True)
    weighted = (tokens.astype(F32) * column_weight).astype(BF16)

    def kmat(index):
        return kall[pl.ds(pl.multiple_of(index * rank, rank), rank), :]

    def mm_k(a, index):
        return lax.dot_general(
            a, kmat(index), (((1,), (1,)), ((), ())), preferred_element_type=F32
        )

    def tspan(index):
        return pl.ds(pl.multiple_of(index * trows, 16), trows)

    def tmat(index):
        return pl.ds(pl.multiple_of(index * rank, rank), rank)

    tpart[...] = jnp.zeros(tpart.shape, BF16)
    tpart[tmat(sec), :] = mm_t(weighted, active[...]).astype(BF16)
    branch[...] = mm_k(weighted, sec)
    for j in range(sections - 1, -1, -1):
        @pl.when(sec == j)
        def _():
            inner[j] = (branch[...] * slope[...]).astype(BF16)
            for lower in range(j):
                sec_copy(CHAIN, inner.at[j], inner.at[j], j, lower).start()

        @pl.when(sec < j)
        def _():
            sec_copy(CHAIN, inner.at[j], inner.at[j], j, j).wait_recv()
            branch[...] += mm_k(inner[j], j)
            tpart[j * rank : (j + 1) * rank, :] = mm_t(inner[j], active[...]).astype(BF16)

    dp_start(TSUM, lambda peer: tpart.at[tspan(peer)], tslots.at[me])
    each_half(lambda peer: half_copy(INNER, inner.at[sec], innerg.at[place], place, peer).start())
    tslots[me] = tpart[tspan(me), :]
    innerg[place] = inner[sec]

    dp_wait(TSUM, lambda peer: tslots.at[peer])
    tsum[tspan(me), :] = lax.fori_loop(
        1, peers, lambda n, total: total + tslots[n].astype(F32), tslots[0].astype(F32)
    ).astype(BF16)
    dp_start(TALL, lambda peer: tsum.at[tspan(me)], tsum.at[tspan(me)])

    local[5].wait()
    local[6].wait()
    for ex, ref in ((INNER, innerg), (XOWN, xg.at[0]), (XFAR, xg.at[1])):
        each_half(lambda peer: half_copy(ex, ref.at[peer], ref.at[peer], peer, peer).wait_recv())
    spread = innerg[...].reshape(half * rows, rank).T
    parts = cross.shape[0]
    span = block // parts
    for part in range(parts):
        held = xg[1, :, :, part * span : (part + 1) * span].reshape(half * rows, span)
        cross[part] = mm(spread, held).astype(BF16)
        far_copy(part).start()

    dp_wait(TALL, lambda peer: tsum.at[tspan(peer)])
    up_out[...] = mm(basis[0], tsum[:rank, :])

    @pl.loop(1, sections)
    def _(n):
        up_out[...] += mm(basis[n], tsum[tmat(n), :])

    for part in range(parts):
        held = xg[0, :, :, part * span : (part + 1) * span].reshape(half * rows, span)
        own = mm(spread, held)
        far_copy(part).wait()
        down_out[part * span : (part + 1) * span, :] = (own + crossg[part].astype(F32)).T

    dp_sent(REP, lambda peer: repg.at[me])
    dp_sent(PRED, lambda peer: pred.at[peer])
    dp_sent(KSUM, lambda peer: kpart.at[kspan(peer)])
    dp_sent(KALL, lambda peer: kall.at[kspan(me)])
    dp_sent(GRAM, lambda peer: gpart)
    dp_sent(WSUM, lambda peer: wpart.at[wspan(peer)])
    dp_sent(WALL, lambda peer: wall.at[wspan(me)])
    for ex, ref in ((INNER, inner.at[sec]), (XOWN, xg.at[0, place]), (XFAR, xg.at[1, place])):
        each_half(lambda peer: half_copy(ex, ref, ref, peer, peer).wait_send())
    dp_sent(TSUM, lambda peer: tpart.at[tspan(peer)])
    dp_sent(TALL, lambda peer: tsum.at[tspan(me)])
    sec_sent(DOWN, basis.at[sec])
    sec_sent(RESID, resid.at[sec])
    for j in range(1, sections):
        @pl.when(sec == j)
        def _():
            for lower in range(j):
                sec_copy(CHAIN, inner.at[j], inner.at[j], lower, lower).wait_send()


def body(
    section_inputs, adapter_down, adapter_up, representation, head_weights, head_targets, head_task
):
    sections = lax.axis_size("section")
    peers = lax.axis_size("dp")
    _, micro, toks, width = section_inputs.shape
    rank = adapter_down.shape[2]
    rows = micro * toks
    block = width // peers
    krows = round_up(-(-sections * rank // peers), 16)
    wrows = round_up(-(-rank // peers), 8)
    half = peers // 2
    parts = max(1, min(4, block // 128))
    trows = round_up(-(-sections * rank // peers), 16)
    vmem = pl.BlockSpec(memory_space=pltpu.VMEM)
    hbm = pl.BlockSpec(memory_space=pltpu.HBM)
    scratch = [
        pltpu.VMEM((rows, width), BF16),
        pltpu.VMEM((width, rank), BF16),
        pltpu.VMEM((block, rank), BF16),
        pltpu.VMEM((sections, block, rank), BF16),
        pltpu.VMEM((peers, toks, block), BF16),
        pltpu.VMEM((2, half, rows, block), BF16),
        pltpu.VMEM((peers, toks, rank), F32),
        pltpu.VMEM((peers, toks, rank), F32),
        pltpu.VMEM((peers * krows, rank), BF16),
        pltpu.VMEM((peers, krows, rank), BF16),
        pltpu.VMEM((peers * krows, rank), BF16),
        pltpu.VMEM((peers * wrows, rank), F32),
        pltpu.VMEM((peers, wrows, rank), F32),
        pltpu.VMEM((peers * wrows, rank), F32),
        pltpu.VMEM((sections, toks, rank), BF16),
        pltpu.VMEM((TASK_ROWS, rank), F32),
        pltpu.VMEM((peers, TASK_ROWS, rank), F32),
        pltpu.VMEM((sections, rows, rank), BF16),
        pltpu.VMEM((half, rows, rank), BF16),
        pltpu.VMEM((peers * trows, rank), BF16),
        pltpu.VMEM((peers, trows, rank), BF16),
        pltpu.VMEM((peers * trows, rank), BF16),
        pltpu.VMEM((rows, rank), BF16),
        pltpu.VMEM((rows, rank), F32),
        pltpu.VMEM((rows, rank), F32),
        pltpu.VMEM((parts, rank, block // parts), BF16),
        pltpu.VMEM((parts, rank, block // parts), BF16),
        pltpu.SemaphoreType.DMA((7,)),
        pltpu.SemaphoreType.DMA((9, peers)),
        pltpu.SemaphoreType.DMA((9, peers)),
        pltpu.SemaphoreType.DMA((3, half)),
        pltpu.SemaphoreType.DMA((3, half)),
        pltpu.SemaphoreType.DMA((parts,)),
        pltpu.SemaphoreType.DMA((parts,)),
        pltpu.SemaphoreType.DMA((3, sections)),
        pltpu.SemaphoreType.DMA((3, sections)),
    ]
    down, up, mix = pl.pallas_call(
        functools.partial(kernel, sections, peers, head_task.shape[0]),
        out_shape=(
            jax.ShapeDtypeStruct((block, rank), F32),
            jax.ShapeDtypeStruct((block, rank), F32),
            jax.ShapeDtypeStruct((TASK_ROWS, rank), F32),
        ),
        in_specs=[hbm] * 5 + [vmem] * 2,
        out_specs=(vmem, vmem, vmem),
        scratch_shapes=scratch,
        compiler_params=pltpu.CompilerParams(
            collective_id=0, has_side_effects=True, vmem_limit_bytes=62 << 20
        ),
    )(
        section_inputs.reshape(rows, width), adapter_down[0], adapter_up[0], representation[0],
        head_weights, head_targets[0], head_task,
    )
    return (down[None], up[None], mix[0, :TASKS])


def solution(mesh):
    in_specs = (
        P("section", None, "dp", None),
        P("section", None, None),
        P("section", None, None),
        P("section", "dp", None),
        P("dp", None),
        P("section", "dp", None),
        P(),
    )
    out_specs = (P("section", "dp", None), P("section", "dp", None), P())
    return jax.shard_map(body, mesh=mesh, in_specs=in_specs, out_specs=out_specs, check_vma=False)
```

```python
import functools

import jax
import jax.numpy as jnp
from jax import lax
from jax.experimental import pallas as pl
from jax.experimental.pallas import tpu as pltpu
from jax.sharding import PartitionSpec as P

TASKS = 6
STEPS = 20
STEP_RATE = 3.0
TASK_ROWS = 8

REP, PRED, KSUM, KALL, WSUM, WALL, GRAM, TSUM, TALL = range(9)
XOWN, XFAR, INNER = range(3)
DOWN, RESID, CHAIN = range(3)

F32 = jnp.float32
BF16 = jnp.bfloat16


def round_up(value, unit):
    return -(-value // unit) * unit


def mm(a, b, precision=None):
    return jnp.dot(a, b, preferred_element_type=F32, precision=precision)


def mm_t(a, b):
    return lax.dot_general(a, b, (((0,), (0,)), ((), ())), preferred_element_type=F32)


def kernel(
    sections, peers, heads,
    x_hbm, down_hbm, up_hbm, rep_hbm, w_hbm, targets, head_task,
    down_out, up_out, mix_out,
    x_buf, down_buf, up_buf, basis, repg, xg, pred, predg, kpart, kslots, kall, wpart, wslots, wall,
    resid, gpart, gslots, inner, innerg, tpart, tslots, tsum, active, slope, branch, cross, crossg,
    local_sem, dp_send, dp_recv, half_send, half_recv, far_send, far_recv, sec_send, sec_recv,
):
    rows, width = x_buf.shape
    rank = down_buf.shape[1]
    block = width // peers
    toks = repg.shape[1]
    krows = kslots.shape[1]
    wrows = wslots.shape[1]
    half = peers // 2
    trows = tslots.shape[1]
    me = lax.axis_index("dp")
    sec = lax.axis_index("section")
    first = lax.div(me, half) * half
    place = me - first
    far = lax.rem(me + half, peers)

    def columns(index):
        return pl.ds(pl.multiple_of(index * block, block), block)

    def blocks(index):
        return pl.ds(pl.multiple_of(index * block, block), block)

    def dp_copy(ex, src, dst, slot, peer):
        return pltpu.make_async_remote_copy(
            src_ref=src, dst_ref=dst, send_sem=dp_send.at[ex, peer], recv_sem=dp_recv.at[ex, slot],
            device_id={"dp": peer}, device_id_type=pl.DeviceIdType.MESH,
        )

    def sec_copy(ex, src, dst, slot, peer):
        return pltpu.make_async_remote_copy(
            src_ref=src, dst_ref=dst, send_sem=sec_send.at[ex, peer], recv_sem=sec_recv.at[ex, slot],
            device_id={"section": peer}, device_id_type=pl.DeviceIdType.MESH,
        )

    def half_copy(ex, src, dst, slot, peer):
        return pltpu.make_async_remote_copy(
            src_ref=src, dst_ref=dst, send_sem=half_send.at[ex, peer], recv_sem=half_recv.at[ex, slot],
            device_id={"dp": first + peer}, device_id_type=pl.DeviceIdType.MESH,
        )

    def far_copy(part):
        return pltpu.make_async_remote_copy(
            src_ref=cross.at[part], dst_ref=crossg.at[part], send_sem=far_send.at[part],
            recv_sem=far_recv.at[part], device_id={"dp": far}, device_id_type=pl.DeviceIdType.MESH,
        )

    def each_half(action):
        @pl.loop(1, half)
        def _(k):
            action(lax.rem(place + k, half))

    def send_inputs(chunk):
        peer = lax.rem(place + 1 + chunk // 2, half)
        if chunk % 2 == 0:
            source = first + peer
            half_copy(XOWN, x_hbm.at[:, columns(source)], xg.at[0, place], place, peer).start()
        else:
            source = lax.rem(first + peer + half, peers)
            half_copy(XFAR, x_hbm.at[:, columns(source)], xg.at[1, place], place, peer).start()

    def each_dp(action):
        @pl.loop(1, peers)
        def _(k):
            action(lax.rem(me + k, peers))

    def each_sec(action):
        @pl.loop(1, sections)
        def _(k):
            action(lax.rem(sec + k, sections))

    def dp_start(ex, src_of, dst):
        each_dp(lambda peer: dp_copy(ex, src_of(peer), dst, me, peer).start())

    def dp_wait(ex, dst_of):
        each_dp(lambda peer: dp_copy(ex, dst_of(peer), dst_of(peer), peer, peer).wait_recv())

    def dp_sent(ex, src_of):
        each_dp(lambda peer: dp_copy(ex, src_of(peer), src_of(peer), peer, peer).wait_send())

    def sec_start(ex, src, dst):
        each_sec(lambda peer: sec_copy(ex, src, dst, sec, peer).start())

    def sec_wait(ex, dst_of):
        each_sec(lambda peer: sec_copy(ex, dst_of(peer), dst_of(peer), peer, peer).wait_recv())

    def sec_sent(ex, src):
        each_sec(lambda peer: sec_copy(ex, src, src, peer, peer).wait_send())

    my_block = blocks(me)
    local = [
        pltpu.make_async_copy(rep_hbm.at[:, columns(me)], repg.at[me], local_sem.at[0]),
        pltpu.make_async_copy(w_hbm, basis.at[sec], local_sem.at[1]),
        pltpu.make_async_copy(x_hbm, x_buf, local_sem.at[2]),
        pltpu.make_async_copy(down_hbm, down_buf, local_sem.at[3]),
        pltpu.make_async_copy(up_hbm.at[my_block], up_buf, local_sem.at[4]),
        pltpu.make_async_copy(x_hbm.at[:, columns(me)], xg.at[0, place], local_sem.at[5]),
        pltpu.make_async_copy(x_hbm.at[:, columns(far)], xg.at[1, place], local_sem.at[6]),
    ]
    for copy in local:
        copy.start()

    barrier = pltpu.get_barrier_semaphore()
    each_dp(lambda peer: pl.semaphore_signal(
        barrier, inc=1, device_id={"dp": peer}, device_id_type=pl.DeviceIdType.MESH))
    each_sec(lambda peer: pl.semaphore_signal(
        barrier, inc=1, device_id={"section": peer}, device_id_type=pl.DeviceIdType.MESH))
    pl.semaphore_wait(barrier, peers + sections - 2)

    dp_start(REP, lambda peer: rep_hbm.at[:, columns(peer)], repg.at[me])
    sec_start(DOWN, down_hbm.at[my_block], basis.at[sec])

    local[1].wait()
    head_block = basis[sec]
    if wpart.shape[0] > rank:
        wpart[rank:, :] = jnp.zeros((wpart.shape[0] - rank, rank), F32)
    wpart[:rank, :] = mm_t(head_block, head_block)

    def wspan(index):
        return pl.ds(pl.multiple_of(index * wrows, 8), wrows)

    dp_start(WSUM, lambda peer: wpart.at[wspan(peer)], wslots.at[me])
    wslots[me] = wpart[wspan(me), :]

    chunks = 2 * (half - 1)
    cuts = [chunks * share // 6 for share in (0, 1, 2, 3, 6)]

    def send_part(part):
        for chunk in range(cuts[part], cuts[part + 1]):
            send_inputs(chunk)

    local[2].wait()
    local[3].wait()

    def add_preact(k, total):
        return total + mm(x_buf[:, columns(k)], down_buf[blocks(k), :])

    preact = lax.fori_loop(0, peers, add_preact, jnp.zeros((rows, rank), F32))
    logistic = jax.nn.sigmoid(preact)
    active[...] = (preact * logistic).astype(BF16)
    slope[...] = logistic * (1.0 + preact * (1.0 - logistic))

    local[0].wait()
    pred[me] = mm(repg[me], head_block)

    @pl.loop(1, peers)
    def _(k):
        peer = lax.rem(me - k + peers, peers)
        dp_copy(REP, repg.at[peer], repg.at[peer], peer, peer).wait_recv()
        pred[peer] = mm(repg[peer], head_block)
        dp_copy(PRED, pred.at[peer], predg.at[me], me, peer).start()

    predg[me] = pred[me]
    dp_wait(WSUM, lambda peer: wslots.at[peer])
    wall[wspan(me), :] = lax.fori_loop(1, peers, lambda n, total: total + wslots[n], wslots[0])
    dp_start(WALL, lambda peer: wall.at[wspan(me)], wall.at[wspan(me)])
    send_part(0)

    local[4].wait()
    sec_wait(DOWN, lambda peer: basis.at[peer])
    used = sections * rank
    if kpart.shape[0] > used:
        kpart[used:, :] = jnp.zeros((kpart.shape[0] - used, rank), BF16)
    up_block = up_buf[...].T
    for j in range(sections):
        kpart[j * rank : (j + 1) * rank, :] = mm(up_block, basis[j]).astype(BF16)

    def kspan(index):
        return pl.ds(pl.multiple_of(index * krows, 16), krows)

    dp_start(KSUM, lambda peer: kpart.at[kspan(peer)], kslots.at[me])
    kslots[me] = kpart[kspan(me), :]

    dp_wait(PRED, lambda peer: predg.at[peer])
    predicted = lax.fori_loop(1, peers, lambda n, total: total + predg[n], predg[0])
    resid[sec] = (predicted - targets[...].astype(F32)).astype(BF16)
    sec_start(RESID, resid.at[sec], resid.at[sec])
    send_part(1)

    dp_wait(KSUM, lambda peer: kslots.at[peer])
    kall[kspan(me), :] = lax.fori_loop(
        1, peers, lambda n, total: total + kslots[n].astype(F32), kslots[0].astype(F32)
    ).astype(BF16)
    dp_start(KALL, lambda peer: kall.at[kspan(me)], kall.at[kspan(me)])

    lanes = lax.broadcasted_iota(jnp.int32, (heads, rank), 1)
    owner = lax.broadcasted_iota(jnp.int32, (heads, rank), 0) * (rank // heads)
    of_head = (lanes >= owner) & (lanes < owner + rank // heads)
    column_task = jnp.sum(
        jnp.where(of_head, head_task[...].astype(F32), 0.0), axis=0, keepdims=True
    )
    wide = lax.broadcasted_iota(jnp.int32, (rank, rank), 0).astype(F32)
    task_wide = (wide == column_task).astype(F32)
    task_tall = task_wide[:TASK_ROWS]

    sec_wait(RESID, lambda peer: resid.at[peer])
    tokens = resid[...].reshape(rows, rank)
    outer = mm_t(tokens, tokens)
    dp_wait(WALL, lambda peer: wall.at[wspan(peer)])
    product = outer * wall[:rank, :]
    picked = mm(task_tall, product, lax.Precision.HIGHEST)
    share = lax.dot_general(
        picked, task_wide, (((1,), (1,)), ((), ())),
        preferred_element_type=F32, precision=lax.Precision.HIGHEST,
    )
    gpart[...] = share
    gslots[me] = share
    dp_start(GRAM, lambda peer: gpart, gslots.at[me])
    send_part(2)
    dp_wait(GRAM, lambda peer: gslots.at[peer])
    gram = lax.fori_loop(1, peers, lambda n, total: total + gslots[n], gslots[0])

    send_part(3)

    down_index = lax.broadcasted_iota(jnp.int32, gram.shape, 0)
    lane_index = lax.broadcasted_iota(jnp.int32, gram.shape, 1)
    trace = jnp.sum(
        jnp.sum(jnp.where(down_index == lane_index, gram, 0.0), axis=1, keepdims=True),
        axis=0, keepdims=True,
    ) + 1e-6
    scaled = gram * (-STEP_RATE / trace)
    tall = jnp.where(down_index[:, :1] < TASKS, 1.0 / TASKS, 0.0).astype(F32)
    flat = jnp.where(lane_index[:1] < TASKS, 1.0 / TASKS, 0.0).astype(F32)
    for _ in range(STEPS):
        along = jnp.sum(scaled * tall, axis=0, keepdims=True)
        across = jnp.sum(scaled * flat, axis=1, keepdims=True)
        tall = tall * jnp.exp(across)
        flat = flat * jnp.exp(along)
        inverse = 1.0 / jnp.sum(tall, axis=0, keepdims=True)
        tall = tall * inverse
        flat = flat * inverse
    mix_out[...] = jnp.broadcast_to(flat, mix_out.shape)

    dp_wait(KALL, lambda peer: kall.at[kspan(peer)])

    column_weight = jnp.sum(task_tall * tall, axis=0, keepdims=True)
    weighted = (tokens.astype(F32) * column_weight).astype(BF16)

    def kmat(index):
        return kall[pl.ds(pl.multiple_of(index * rank, rank), rank), :]

    def mm_k(a, index):
        return lax.dot_general(
            a, kmat(index), (((1,), (1,)), ((), ())), preferred_element_type=F32
        )

    def tspan(index):
        return pl.ds(pl.multiple_of(index * trows, 16), trows)

    def tmat(index):
        return pl.ds(pl.multiple_of(index * rank, rank), rank)

    tpart[...] = jnp.zeros(tpart.shape, BF16)
    tpart[tmat(sec), :] = mm_t(weighted, active[...]).astype(BF16)
    branch[...] = mm_k(weighted, sec)
    for j in range(sections - 1, -1, -1):
        @pl.when(sec == j)
        def _():
            inner[j] = (branch[...] * slope[...]).astype(BF16)
            for lower in range(j):
                sec_copy(CHAIN, inner.at[j], inner.at[j], j, lower).start()

        @pl.when(sec < j)
        def _():
            sec_copy(CHAIN, inner.at[j], inner.at[j], j, j).wait_recv()
            branch[...] += mm_k(inner[j], j)
            tpart[j * rank : (j + 1) * rank, :] = mm_t(inner[j], active[...]).astype(BF16)

    each_half(lambda peer: half_copy(INNER, inner.at[sec], innerg.at[place], place, peer).start())
    dp_start(TSUM, lambda peer: tpart.at[tspan(peer)], tslots.at[me])
    tslots[me] = tpart[tspan(me), :]
    innerg[place] = inner[sec]

    local[5].wait()
    local[6].wait()
    for ex, ref in ((INNER, innerg), (XOWN, xg.at[0]), (XFAR, xg.at[1])):
        each_half(lambda peer: half_copy(ex, ref.at[peer], ref.at[peer], peer, peer).wait_recv())
    spread = innerg[...].reshape(half * rows, rank).T
    parts = cross.shape[0]
    span = block // parts
    for part in range(parts):
        held = xg[1, :, :, part * span : (part + 1) * span].reshape(half * rows, span)
        cross[part] = mm(spread, held).astype(BF16)
        far_copy(part).start()
        if part == 0:
            dp_wait(TSUM, lambda peer: tslots.at[peer])
            tsum[tspan(me), :] = lax.fori_loop(
                1, peers, lambda n, total: total + tslots[n].astype(F32), tslots[0].astype(F32)
            ).astype(BF16)
            dp_start(TALL, lambda peer: tsum.at[tspan(me)], tsum.at[tspan(me)])

    dp_wait(TALL, lambda peer: tsum.at[tspan(peer)])
    up_out[...] = mm(basis[0], tsum[:rank, :])

    @pl.loop(1, sections)
    def _(n):
        up_out[...] += mm(basis[n], tsum[tmat(n), :])

    for part in range(parts):
        held = xg[0, :, :, part * span : (part + 1) * span].reshape(half * rows, span)
        own = mm(spread, held)
        far_copy(part).wait()
        down_out[part * span : (part + 1) * span, :] = (own + crossg[part].astype(F32)).T

    dp_sent(REP, lambda peer: repg.at[me])
    dp_sent(PRED, lambda peer: pred.at[peer])
    dp_sent(KSUM, lambda peer: kpart.at[kspan(peer)])
    dp_sent(KALL, lambda peer: kall.at[kspan(me)])
    dp_sent(GRAM, lambda peer: gpart)
    dp_sent(WSUM, lambda peer: wpart.at[wspan(peer)])
    dp_sent(WALL, lambda peer: wall.at[wspan(me)])
    for ex, ref in ((INNER, inner.at[sec]), (XOWN, xg.at[0, place]), (XFAR, xg.at[1, place])):
        each_half(lambda peer: half_copy(ex, ref, ref, peer, peer).wait_send())
    dp_sent(TSUM, lambda peer: tpart.at[tspan(peer)])
    dp_sent(TALL, lambda peer: tsum.at[tspan(me)])
    sec_sent(DOWN, basis.at[sec])
    sec_sent(RESID, resid.at[sec])
    for j in range(1, sections):
        @pl.when(sec == j)
        def _():
            for lower in range(j):
                sec_copy(CHAIN, inner.at[j], inner.at[j], lower, lower).wait_send()


def body(
    section_inputs, adapter_down, adapter_up, representation, head_weights, head_targets, head_task
):
    sections = lax.axis_size("section")
    peers = lax.axis_size("dp")
    _, micro, toks, width = section_inputs.shape
    rank = adapter_down.shape[2]
    rows = micro * toks
    block = width // peers
    krows = round_up(-(-sections * rank // peers), 16)
    wrows = round_up(-(-rank // peers), 8)
    half = peers // 2
    parts = max(1, min(4, block // 128))
    trows = round_up(-(-sections * rank // peers), 16)
    vmem = pl.BlockSpec(memory_space=pltpu.VMEM)
    hbm = pl.BlockSpec(memory_space=pltpu.HBM)
    scratch = [
        pltpu.VMEM((rows, width), BF16),
        pltpu.VMEM((width, rank), BF16),
        pltpu.VMEM((block, rank), BF16),
        pltpu.VMEM((sections, block, rank), BF16),
        pltpu.VMEM((peers, toks, block), BF16),
        pltpu.VMEM((2, half, rows, block), BF16),
        pltpu.VMEM((peers, toks, rank), F32),
        pltpu.VMEM((peers, toks, rank), F32),
        pltpu.VMEM((peers * krows, rank), BF16),
        pltpu.VMEM((peers, krows, rank), BF16),
        pltpu.VMEM((peers * krows, rank), BF16),
        pltpu.VMEM((peers * wrows, rank), F32),
        pltpu.VMEM((peers, wrows, rank), F32),
        pltpu.VMEM((peers * wrows, rank), F32),
        pltpu.VMEM((sections, toks, rank), BF16),
        pltpu.VMEM((TASK_ROWS, rank), F32),
        pltpu.VMEM((peers, TASK_ROWS, rank), F32),
        pltpu.VMEM((sections, rows, rank), BF16),
        pltpu.VMEM((half, rows, rank), BF16),
        pltpu.VMEM((peers * trows, rank), BF16),
        pltpu.VMEM((peers, trows, rank), BF16),
        pltpu.VMEM((peers * trows, rank), BF16),
        pltpu.VMEM((rows, rank), BF16),
        pltpu.VMEM((rows, rank), F32),
        pltpu.VMEM((rows, rank), F32),
        pltpu.VMEM((parts, rank, block // parts), BF16),
        pltpu.VMEM((parts, rank, block // parts), BF16),
        pltpu.SemaphoreType.DMA((7,)),
        pltpu.SemaphoreType.DMA((9, peers)),
        pltpu.SemaphoreType.DMA((9, peers)),
        pltpu.SemaphoreType.DMA((3, half)),
        pltpu.SemaphoreType.DMA((3, half)),
        pltpu.SemaphoreType.DMA((parts,)),
        pltpu.SemaphoreType.DMA((parts,)),
        pltpu.SemaphoreType.DMA((3, sections)),
        pltpu.SemaphoreType.DMA((3, sections)),
    ]
    down, up, mix = pl.pallas_call(
        functools.partial(kernel, sections, peers, head_task.shape[0]),
        out_shape=(
            jax.ShapeDtypeStruct((block, rank), F32),
            jax.ShapeDtypeStruct((block, rank), F32),
            jax.ShapeDtypeStruct((TASK_ROWS, rank), F32),
        ),
        in_specs=[hbm] * 5 + [vmem] * 2,
        out_specs=(vmem, vmem, vmem),
        scratch_shapes=scratch,
        compiler_params=pltpu.CompilerParams(
            collective_id=0, has_side_effects=True, vmem_limit_bytes=62 << 20
        ),
    )(
        section_inputs.reshape(rows, width), adapter_down[0], adapter_up[0], representation[0],
        head_weights, head_targets[0], head_task,
    )
    return (down[None], up[None], mix[0, :TASKS])


def solution(mesh):
    in_specs = (
        P("section", None, "dp", None),
        P("section", None, None),
        P("section", None, None),
        P("section", "dp", None),
        P("dp", None),
        P("section", "dp", None),
        P(),
    )
    out_specs = (P("section", "dp", None), P("section", "dp", None), P())
    return jax.shard_map(body, mesh=mesh, in_specs=in_specs, out_specs=out_specs, check_vma=False)
```

```python
import functools

import jax
import jax.numpy as jnp
from jax import lax
from jax.experimental import pallas as pl
from jax.experimental.pallas import tpu as pltpu
from jax.sharding import PartitionSpec as P

TASKS = 6
STEPS = 20
STEP_RATE = 3.0
TASK_ROWS = 8

REP, PRED, KSUM, KALL, WSUM, WALL, GRAM, TSUM, TALL = range(9)
XOWN, XFAR, INNER = range(3)
DOWN, RESID, CHAIN = range(3)

F32 = jnp.float32
BF16 = jnp.bfloat16


def round_up(value, unit):
    return -(-value // unit) * unit


def mm(a, b, precision=None):
    return jnp.dot(a, b, preferred_element_type=F32, precision=precision)


def mm_t(a, b):
    return lax.dot_general(a, b, (((0,), (0,)), ((), ())), preferred_element_type=F32)


def kernel(
    sections, peers, heads,
    x_hbm, down_hbm, up_hbm, rep_hbm, w_hbm, targets, head_task,
    down_out, up_out, mix_out,
    x_buf, down_buf, up_buf, basis, repg, xg, pred, predg, kpart, kslots, kall, wpart, wslots, wall,
    resid, gpart, gslots, inner, innerg, tpart, tslots, tsum, active, slope, branch, cross, crossg,
    local_sem, dp_send, dp_recv, half_send, half_recv, far_send, far_recv, sec_send, sec_recv,
):
    rows, width = x_buf.shape
    rank = down_buf.shape[1]
    block = width // peers
    toks = repg.shape[1]
    krows = kslots.shape[1]
    wrows = wslots.shape[1]
    half = peers // 2
    trows = tslots.shape[1]
    me = lax.axis_index("dp")
    sec = lax.axis_index("section")
    first = lax.div(me, half) * half
    place = me - first
    far = lax.rem(me + half, peers)

    def columns(index):
        return pl.ds(pl.multiple_of(index * block, block), block)

    def blocks(index):
        return pl.ds(pl.multiple_of(index * block, block), block)

    def dp_copy(ex, src, dst, slot, peer):
        return pltpu.make_async_remote_copy(
            src_ref=src, dst_ref=dst, send_sem=dp_send.at[ex, peer], recv_sem=dp_recv.at[ex, slot],
            device_id={"dp": peer}, device_id_type=pl.DeviceIdType.MESH,
        )

    def sec_copy(ex, src, dst, slot, peer):
        return pltpu.make_async_remote_copy(
            src_ref=src, dst_ref=dst, send_sem=sec_send.at[ex, peer], recv_sem=sec_recv.at[ex, slot],
            device_id={"section": peer}, device_id_type=pl.DeviceIdType.MESH,
        )

    def half_copy(ex, src, dst, slot, peer):
        return pltpu.make_async_remote_copy(
            src_ref=src, dst_ref=dst, send_sem=half_send.at[ex, peer], recv_sem=half_recv.at[ex, slot],
            device_id={"dp": first + peer}, device_id_type=pl.DeviceIdType.MESH,
        )

    def far_copy(part):
        return pltpu.make_async_remote_copy(
            src_ref=cross.at[part], dst_ref=crossg.at[part], send_sem=far_send.at[part],
            recv_sem=far_recv.at[part], device_id={"dp": far}, device_id_type=pl.DeviceIdType.MESH,
        )

    def each_half(action):
        @pl.loop(1, half)
        def _(k):
            action(lax.rem(place + k, half))

    def send_inputs(chunk):
        peer = lax.rem(place + 1 + chunk % (half - 1), half)
        if chunk >= half - 1:
            source = first + peer
            half_copy(XOWN, x_hbm.at[:, columns(source)], xg.at[0, place], place, peer).start()
        else:
            source = lax.rem(first + peer + half, peers)
            half_copy(XFAR, x_hbm.at[:, columns(source)], xg.at[1, place], place, peer).start()

    def each_dp(action):
        @pl.loop(1, peers)
        def _(k):
            action(lax.rem(me + k, peers))

    def each_sec(action):
        @pl.loop(1, sections)
        def _(k):
            action(lax.rem(sec + k, sections))

    def dp_start(ex, src_of, dst):
        each_dp(lambda peer: dp_copy(ex, src_of(peer), dst, me, peer).start())

    def dp_wait(ex, dst_of):
        each_dp(lambda peer: dp_copy(ex, dst_of(peer), dst_of(peer), peer, peer).wait_recv())

    def dp_sent(ex, src_of):
        each_dp(lambda peer: dp_copy(ex, src_of(peer), src_of(peer), peer, peer).wait_send())

    def sec_start(ex, src, dst):
        each_sec(lambda peer: sec_copy(ex, src, dst, sec, peer).start())

    def sec_wait(ex, dst_of):
        each_sec(lambda peer: sec_copy(ex, dst_of(peer), dst_of(peer), peer, peer).wait_recv())

    def sec_sent(ex, src):
        each_sec(lambda peer: sec_copy(ex, src, src, peer, peer).wait_send())

    my_block = blocks(me)
    local = [
        pltpu.make_async_copy(rep_hbm.at[:, columns(me)], repg.at[me], local_sem.at[0]),
        pltpu.make_async_copy(w_hbm, basis.at[sec], local_sem.at[1]),
        pltpu.make_async_copy(x_hbm, x_buf, local_sem.at[2]),
        pltpu.make_async_copy(down_hbm, down_buf, local_sem.at[3]),
        pltpu.make_async_copy(up_hbm.at[my_block], up_buf, local_sem.at[4]),
        pltpu.make_async_copy(x_hbm.at[:, columns(me)], xg.at[0, place], local_sem.at[5]),
        pltpu.make_async_copy(x_hbm.at[:, columns(far)], xg.at[1, place], local_sem.at[6]),
    ]
    for copy in local:
        copy.start()

    barrier = pltpu.get_barrier_semaphore()
    each_dp(lambda peer: pl.semaphore_signal(
        barrier, inc=1, device_id={"dp": peer}, device_id_type=pl.DeviceIdType.MESH))
    each_sec(lambda peer: pl.semaphore_signal(
        barrier, inc=1, device_id={"section": peer}, device_id_type=pl.DeviceIdType.MESH))
    pl.semaphore_wait(barrier, peers + sections - 2)

    dp_start(REP, lambda peer: rep_hbm.at[:, columns(peer)], repg.at[me])
    sec_start(DOWN, down_hbm.at[my_block], basis.at[sec])

    local[1].wait()
    head_block = basis[sec]
    if wpart.shape[0] > rank:
        wpart[rank:, :] = jnp.zeros((wpart.shape[0] - rank, rank), F32)
    wpart[:rank, :] = mm_t(head_block, head_block)

    def wspan(index):
        return pl.ds(pl.multiple_of(index * wrows, 8), wrows)

    dp_start(WSUM, lambda peer: wpart.at[wspan(peer)], wslots.at[me])
    wslots[me] = wpart[wspan(me), :]

    chunks = 2 * (half - 1)
    cuts = [chunks * share // 6 for share in (0, 1, 2, 3, 6)]

    def send_part(part):
        for chunk in range(cuts[part], cuts[part + 1]):
            send_inputs(chunk)

    local[2].wait()
    local[3].wait()

    def add_preact(k, total):
        return total + mm(x_buf[:, columns(k)], down_buf[blocks(k), :])

    preact = lax.fori_loop(0, peers, add_preact, jnp.zeros((rows, rank), F32))
    logistic = jax.nn.sigmoid(preact)
    active[...] = (preact * logistic).astype(BF16)
    slope[...] = logistic * (1.0 + preact * (1.0 - logistic))

    local[0].wait()
    pred[me] = mm(repg[me], head_block)

    @pl.loop(1, peers)
    def _(k):
        peer = lax.rem(me - k + peers, peers)
        dp_copy(REP, repg.at[peer], repg.at[peer], peer, peer).wait_recv()
        pred[peer] = mm(repg[peer], head_block)
        dp_copy(PRED, pred.at[peer], predg.at[me], me, peer).start()

    predg[me] = pred[me]
    dp_wait(WSUM, lambda peer: wslots.at[peer])
    wall[wspan(me), :] = lax.fori_loop(1, peers, lambda n, total: total + wslots[n], wslots[0])
    dp_start(WALL, lambda peer: wall.at[wspan(me)], wall.at[wspan(me)])
    send_part(0)

    local[4].wait()
    sec_wait(DOWN, lambda peer: basis.at[peer])
    used = sections * rank
    if kpart.shape[0] > used:
        kpart[used:, :] = jnp.zeros((kpart.shape[0] - used, rank), BF16)
    up_block = up_buf[...].T
    for j in range(sections):
        kpart[j * rank : (j + 1) * rank, :] = mm(up_block, basis[j]).astype(BF16)

    def kspan(index):
        return pl.ds(pl.multiple_of(index * krows, 16), krows)

    dp_start(KSUM, lambda peer: kpart.at[kspan(peer)], kslots.at[me])
    kslots[me] = kpart[kspan(me), :]

    dp_wait(PRED, lambda peer: predg.at[peer])
    predicted = lax.fori_loop(1, peers, lambda n, total: total + predg[n], predg[0])
    resid[sec] = (predicted - targets[...].astype(F32)).astype(BF16)
    sec_start(RESID, resid.at[sec], resid.at[sec])
    send_part(1)

    dp_wait(KSUM, lambda peer: kslots.at[peer])
    kall[kspan(me), :] = lax.fori_loop(
        1, peers, lambda n, total: total + kslots[n].astype(F32), kslots[0].astype(F32)
    ).astype(BF16)
    dp_start(KALL, lambda peer: kall.at[kspan(me)], kall.at[kspan(me)])

    lanes = lax.broadcasted_iota(jnp.int32, (heads, rank), 1)
    owner = lax.broadcasted_iota(jnp.int32, (heads, rank), 0) * (rank // heads)
    of_head = (lanes >= owner) & (lanes < owner + rank // heads)
    column_task = jnp.sum(
        jnp.where(of_head, head_task[...].astype(F32), 0.0), axis=0, keepdims=True
    )
    wide = lax.broadcasted_iota(jnp.int32, (rank, rank), 0).astype(F32)
    task_wide = (wide == column_task).astype(F32)
    task_tall = task_wide[:TASK_ROWS]

    sec_wait(RESID, lambda peer: resid.at[peer])
    tokens = resid[...].reshape(rows, rank)
    outer = mm_t(tokens, tokens)
    dp_wait(WALL, lambda peer: wall.at[wspan(peer)])
    product = outer * wall[:rank, :]
    picked = mm(task_tall, product, lax.Precision.HIGHEST)
    share = lax.dot_general(
        picked, task_wide, (((1,), (1,)), ((), ())),
        preferred_element_type=F32, precision=lax.Precision.HIGHEST,
    )
    gpart[...] = share
    gslots[me] = share
    dp_start(GRAM, lambda peer: gpart, gslots.at[me])
    send_part(2)
    dp_wait(GRAM, lambda peer: gslots.at[peer])
    gram = lax.fori_loop(1, peers, lambda n, total: total + gslots[n], gslots[0])

    send_part(3)

    down_index = lax.broadcasted_iota(jnp.int32, gram.shape, 0)
    lane_index = lax.broadcasted_iota(jnp.int32, gram.shape, 1)
    trace = jnp.sum(
        jnp.sum(jnp.where(down_index == lane_index, gram, 0.0), axis=1, keepdims=True),
        axis=0, keepdims=True,
    ) + 1e-6
    scaled = gram * (-STEP_RATE / trace)
    tall = jnp.where(down_index[:, :1] < TASKS, 1.0 / TASKS, 0.0).astype(F32)
    flat = jnp.where(lane_index[:1] < TASKS, 1.0 / TASKS, 0.0).astype(F32)
    for _ in range(STEPS):
        along = jnp.sum(scaled * tall, axis=0, keepdims=True)
        across = jnp.sum(scaled * flat, axis=1, keepdims=True)
        tall = tall * jnp.exp(across)
        flat = flat * jnp.exp(along)
        inverse = 1.0 / jnp.sum(tall, axis=0, keepdims=True)
        tall = tall * inverse
        flat = flat * inverse
    mix_out[...] = jnp.broadcast_to(flat, mix_out.shape)

    dp_wait(KALL, lambda peer: kall.at[kspan(peer)])

    column_weight = jnp.sum(task_tall * tall, axis=0, keepdims=True)
    weighted = (tokens.astype(F32) * column_weight).astype(BF16)

    def kmat(index):
        return kall[pl.ds(pl.multiple_of(index * rank, rank), rank), :]

    def mm_k(a, index):
        return lax.dot_general(
            a, kmat(index), (((1,), (1,)), ((), ())), preferred_element_type=F32
        )

    def tspan(index):
        return pl.ds(pl.multiple_of(index * trows, 16), trows)

    def tmat(index):
        return pl.ds(pl.multiple_of(index * rank, rank), rank)

    tpart[...] = jnp.zeros(tpart.shape, BF16)
    tpart[tmat(sec), :] = mm_t(weighted, active[...]).astype(BF16)
    branch[...] = mm_k(weighted, sec)
    for j in range(sections - 1, -1, -1):
        @pl.when(sec == j)
        def _():
            inner[j] = (branch[...] * slope[...]).astype(BF16)
            for lower in range(j):
                sec_copy(CHAIN, inner.at[j], inner.at[j], j, lower).start()

        @pl.when(sec < j)
        def _():
            sec_copy(CHAIN, inner.at[j], inner.at[j], j, j).wait_recv()
            branch[...] += mm_k(inner[j], j)
            tpart[j * rank : (j + 1) * rank, :] = mm_t(inner[j], active[...]).astype(BF16)

    each_half(lambda peer: half_copy(INNER, inner.at[sec], innerg.at[place], place, peer).start())
    dp_start(TSUM, lambda peer: tpart.at[tspan(peer)], tslots.at[me])
    tslots[me] = tpart[tspan(me), :]
    innerg[place] = inner[sec]

    local[6].wait()
    for ex, ref in ((INNER, innerg), (XFAR, xg.at[1])):
        each_half(lambda peer: half_copy(ex, ref.at[peer], ref.at[peer], peer, peer).wait_recv())
    spread = innerg[...].reshape(half * rows, rank).T
    parts = cross.shape[0]
    span = block // parts
    for part in range(parts):
        held = xg[1, :, :, part * span : (part + 1) * span].reshape(half * rows, span)
        cross[part] = mm(spread, held).astype(BF16)
        far_copy(part).start()
        if part == 0:
            dp_wait(TSUM, lambda peer: tslots.at[peer])
            tsum[tspan(me), :] = lax.fori_loop(
                1, peers, lambda n, total: total + tslots[n].astype(F32), tslots[0].astype(F32)
            ).astype(BF16)
            dp_start(TALL, lambda peer: tsum.at[tspan(me)], tsum.at[tspan(me)])

    dp_wait(TALL, lambda peer: tsum.at[tspan(peer)])
    up_out[...] = mm(basis[0], tsum[:rank, :])

    @pl.loop(1, sections)
    def _(n):
        up_out[...] += mm(basis[n], tsum[tmat(n), :])

    local[5].wait()
    each_half(
        lambda peer: half_copy(XOWN, xg.at[0, peer], xg.at[0, peer], peer, peer).wait_recv()
    )
    for part in range(parts):
        held = xg[0, :, :, part * span : (part + 1) * span].reshape(half * rows, span)
        own = mm(spread, held)
        far_copy(part).wait()
        down_out[part * span : (part + 1) * span, :] = (own + crossg[part].astype(F32)).T

    dp_sent(REP, lambda peer: repg.at[me])
    dp_sent(PRED, lambda peer: pred.at[peer])
    dp_sent(KSUM, lambda peer: kpart.at[kspan(peer)])
    dp_sent(KALL, lambda peer: kall.at[kspan(me)])
    dp_sent(GRAM, lambda peer: gpart)
    dp_sent(WSUM, lambda peer: wpart.at[wspan(peer)])
    dp_sent(WALL, lambda peer: wall.at[wspan(me)])
    for ex, ref in ((INNER, inner.at[sec]), (XOWN, xg.at[0, place]), (XFAR, xg.at[1, place])):
        each_half(lambda peer: half_copy(ex, ref, ref, peer, peer).wait_send())
    dp_sent(TSUM, lambda peer: tpart.at[tspan(peer)])
    dp_sent(TALL, lambda peer: tsum.at[tspan(me)])
    sec_sent(DOWN, basis.at[sec])
    sec_sent(RESID, resid.at[sec])
    for j in range(1, sections):
        @pl.when(sec == j)
        def _():
            for lower in range(j):
                sec_copy(CHAIN, inner.at[j], inner.at[j], lower, lower).wait_send()


def body(
    section_inputs, adapter_down, adapter_up, representation, head_weights, head_targets, head_task
):
    sections = lax.axis_size("section")
    peers = lax.axis_size("dp")
    _, micro, toks, width = section_inputs.shape
    rank = adapter_down.shape[2]
    rows = micro * toks
    block = width // peers
    krows = round_up(-(-sections * rank // peers), 16)
    wrows = round_up(-(-rank // peers), 8)
    half = peers // 2
    parts = max(1, min(4, block // 128))
    trows = round_up(-(-sections * rank // peers), 16)
    vmem = pl.BlockSpec(memory_space=pltpu.VMEM)
    hbm = pl.BlockSpec(memory_space=pltpu.HBM)
    scratch = [
        pltpu.VMEM((rows, width), BF16),
        pltpu.VMEM((width, rank), BF16),
        pltpu.VMEM((block, rank), BF16),
        pltpu.VMEM((sections, block, rank), BF16),
        pltpu.VMEM((peers, toks, block), BF16),
        pltpu.VMEM((2, half, rows, block), BF16),
        pltpu.VMEM((peers, toks, rank), F32),
        pltpu.VMEM((peers, toks, rank), F32),
        pltpu.VMEM((peers * krows, rank), BF16),
        pltpu.VMEM((peers, krows, rank), BF16),
        pltpu.VMEM((peers * krows, rank), BF16),
        pltpu.VMEM((peers * wrows, rank), F32),
        pltpu.VMEM((peers, wrows, rank), F32),
        pltpu.VMEM((peers * wrows, rank), F32),
        pltpu.VMEM((sections, toks, rank), BF16),
        pltpu.VMEM((TASK_ROWS, rank), F32),
        pltpu.VMEM((peers, TASK_ROWS, rank), F32),
        pltpu.VMEM((sections, rows, rank), BF16),
        pltpu.VMEM((half, rows, rank), BF16),
        pltpu.VMEM((peers * trows, rank), BF16),
        pltpu.VMEM((peers, trows, rank), BF16),
        pltpu.VMEM((peers * trows, rank), BF16),
        pltpu.VMEM((rows, rank), BF16),
        pltpu.VMEM((rows, rank), F32),
        pltpu.VMEM((rows, rank), F32),
        pltpu.VMEM((parts, rank, block // parts), BF16),
        pltpu.VMEM((parts, rank, block // parts), BF16),
        pltpu.SemaphoreType.DMA((7,)),
        pltpu.SemaphoreType.DMA((9, peers)),
        pltpu.SemaphoreType.DMA((9, peers)),
        pltpu.SemaphoreType.DMA((3, half)),
        pltpu.SemaphoreType.DMA((3, half)),
        pltpu.SemaphoreType.DMA((parts,)),
        pltpu.SemaphoreType.DMA((parts,)),
        pltpu.SemaphoreType.DMA((3, sections)),
        pltpu.SemaphoreType.DMA((3, sections)),
    ]
    down, up, mix = pl.pallas_call(
        functools.partial(kernel, sections, peers, head_task.shape[0]),
        out_shape=(
            jax.ShapeDtypeStruct((block, rank), F32),
            jax.ShapeDtypeStruct((block, rank), F32),
            jax.ShapeDtypeStruct((TASK_ROWS, rank), F32),
        ),
        in_specs=[hbm] * 5 + [vmem] * 2,
        out_specs=(vmem, vmem, vmem),
        scratch_shapes=scratch,
        compiler_params=pltpu.CompilerParams(
            collective_id=0, has_side_effects=True, vmem_limit_bytes=62 << 20
        ),
    )(
        section_inputs.reshape(rows, width), adapter_down[0], adapter_up[0], representation[0],
        head_weights, head_targets[0], head_task,
    )
    return (down[None], up[None], mix[0, :TASKS])


def solution(mesh):
    in_specs = (
        P("section", None, "dp", None),
        P("section", None, None),
        P("section", None, None),
        P("section", "dp", None),
        P("dp", None),
        P("section", "dp", None),
        P(),
    )
    out_specs = (P("section", "dp", None), P("section", "dp", None), P())
    return jax.shard_map(body, mesh=mesh, in_specs=in_specs, out_specs=out_specs, check_vma=False)
```
